32 devices in a mesh: parts: 2 (over x), row: 8 (over z, y), col: 2 (over core).
Axes of the slice: x: 2, y: 2, z: 4, core: 2. Of those that a mesh axis runs over, the one named last changes fastest.
Arguments:
- tokens: bfloat16 [64, 512, 512], P(('parts', 'row'), 'col'), parts along dimension 0, may hold values from -6 to 6
- expand_weight: bfloat16 [512, 2048], replicated, may hold values from -0.25 to 0.25
- depth_kernel: float32 [3, 3, 2048], replicated, may hold values from -2 to 2
- project_weight: bfloat16 [2048, 512], replicated, may hold values from -0.125 to 0.125
- norm_gain: float32 [512], replicated, may hold values from 0.25 to 1.75
- attend_weight: bfloat16 [512, 1536], replicated, may hold values from -3 to 3
- output_weight: bfloat16 [512, 512], replicated, may hold values from -0.25 to 0.25
Outputs:
- section_out: bfloat16 [64, 512, 512], P(('parts', 'row'), 'col'), parts along dimension 0
The draws below stay inside these ranges and needn't reach their ends.
There are 2 independent parts, one for each index of `parts`. The reference program is written for one: setup_inputs(seed, part) draws one part's arguments, and reference() takes and returns one part's arrays. A program takes and returns all parts, laid end to end along the dimension named above; an argument that names none is the same for every part. Nothing has to cross between parts.
All inputs are finite; a program needn't handle non-finite values.
Results may differ from the reference program's by a relative error of at most 0.012.
Values may be sent and summed in bfloat16 or wider, within the bound.
A program may use at most 128 MiB of HBM per device.

```python
import math
import jax
import jax.numpy as jnp
from jax import lax

C = 512
HID = 2048
HEADS = 16
HEAD_DIM = 32
GRID = 16
TILE_ROWS = 4
H = 32
W = 512


def draw_attend_weight(key, part):
    first, second, third = jax.random.split(key, 3)
    queries = jax.random.normal(first, (C, C), jnp.float32) * 1.5 / math.sqrt(C)
    keyed = jax.random.normal(second, (C, C), jnp.float32) * 1.5 / math.sqrt(C)
    values = jax.random.normal(third, (C, C), jnp.float32) * 2.0 / math.sqrt(C)
    whole = jnp.concatenate([queries, keyed, values], axis=1)
    return jnp.clip(whole, -3.0, 3.0).astype(jnp.bfloat16)


def shard_levels(rng, dims, cuts, low, largest):
    level, own = 1.0, jax.random.fold_in(rng, 6)
    for axis_at, parts in cuts:
        steps = jnp.exp(jax.random.uniform(jax.random.fold_in(own, axis_at), (parts,), jnp.float32, low / len(cuts), largest / len(cuts)))
        level = level * jnp.repeat(steps, dims[axis_at] // parts).reshape([-1 if axis == axis_at else 1 for axis in range(len(dims))])
    return level


def noise(own_key, dims, scale, limit, cuts=(), kind=jnp.bfloat16):
    level = shard_levels(own_key, dims, cuts, -0.22, 0.18) if cuts else 1.0
    values = jax.random.normal(own_key, dims, jnp.float32) * scale * level
    return jnp.minimum(jnp.maximum(values, -limit), limit).astype(kind)


def setup_inputs(seed: int = 0, part: int = 0) -> dict:
    keys = jax.random.split(jax.random.key(seed), 8)
    part_keys = jax.random.split(jax.random.fold_in(keys[7], part), 8)
    return {
        "tokens": noise(part_keys[0], (H, W, C), 1.0, 6.0, ((0, 8), (1, 2))),
        "expand_weight": noise(keys[1], (C, HID), C ** -0.5, 0.25),
        "depth_kernel": noise(keys[2], (3, 3, HID), 9 ** -0.5, 2.0, (), jnp.float32),
        "project_weight": noise(keys[3], (HID, C), HID ** -0.5, 0.125),
        "norm_gain": jnp.clip(1.0 + 0.15 * jax.random.normal(keys[4], (C,), jnp.float32), 0.25, 1.75),
        "attend_weight": draw_attend_weight(jax.random.fold_in(keys[7], 71), part),
        "output_weight": noise(keys[6], (C, C), C ** -0.5, 0.25),
    }


def gelu_tanh(values):
    return jax.nn.gelu(values, approximate=True)

def mbconv_region(tokens, expand_weight, depth_kernel, project_weight):
    height, width, channels = tokens.shape
    padded = jnp.pad(tokens, ((1, 1), (1, 1), (0, 0)))
    block = TILE_ROWS

    def one_block(index):
        start = (index * block).astype(jnp.int32)
        window = lax.dynamic_slice_in_dim(padded, start, block + 2, 0)
        product = jnp.dot(window.reshape(-1, channels), expand_weight, preferred_element_type=jnp.float32)
        expanded = gelu_tanh(product).astype(jnp.bfloat16).reshape(block + 2, width + 2, -1)
        total = jnp.zeros((block, width, expanded.shape[2]), jnp.float32)
        for shift_row in range(3):
            for shift_col in range(3):
                total = total + expanded[shift_row:shift_row + block, shift_col:shift_col + width].astype(jnp.float32) * depth_kernel[shift_row, shift_col]
        depth = gelu_tanh(total).astype(jnp.bfloat16)
        center = lax.dynamic_slice_in_dim(tokens, start, block, 0)
        branch = jnp.dot(depth.reshape(block * width, -1), project_weight, preferred_element_type=jnp.float32)
        return (center.astype(jnp.float32) + branch.reshape(block, width, channels)).astype(jnp.bfloat16)
    blocks = lax.map(one_block, jnp.arange(height // block, dtype=jnp.int32))
    return blocks.reshape(height, width, channels)

def layer_norm(values, gain):
    values = values.astype(jnp.float32)
    center = lax.optimization_barrier(jnp.mean(values, axis=-1, keepdims=True))
    spread = lax.optimization_barrier(jnp.mean((values - center) ** 2, axis=-1, keepdims=True))
    return ((values - center) * lax.rsqrt(spread + 1e-05) * gain).astype(jnp.bfloat16)

def attend_groups(groups, attend_weight, output_weight):
    count, members, channels = groups.shape
    projected = jnp.dot(groups.reshape(count * members, channels), attend_weight, preferred_element_type=jnp.float32)
    projected = projected.astype(jnp.bfloat16).reshape(count, members, 3, HEADS, HEAD_DIM)
    query_heads = projected[:, :, 0].astype(jnp.float32)
    key_heads = projected[:, :, 1].astype(jnp.float32)
    value_heads = projected[:, :, 2].astype(jnp.float32)
    scores = jnp.einsum('nqhd,nkhd->nhqk', query_heads, key_heads) / math.sqrt(HEAD_DIM)
    soft = jax.nn.softmax(scores, axis=-1).astype(jnp.bfloat16)
    heads_out = jnp.einsum('nhqk,nkhd->nqhd', soft.astype(jnp.float32), value_heads)
    heads_out = heads_out.astype(jnp.bfloat16).reshape(count * members, channels)
    result = jnp.dot(heads_out, output_weight, preferred_element_type=jnp.float32).astype(jnp.bfloat16)
    return result.reshape(count, members, channels)

def reference(tokens, expand_weight, depth_kernel, project_weight, norm_gain, attend_weight, output_weight):
    height, width, channels = tokens.shape
    mbconv = mbconv_region(tokens, expand_weight, depth_kernel, project_weight)
    normed = layer_norm(mbconv, norm_gain)
    stride_rows = height // GRID
    stride_cols = width // GRID
    grouped = normed.reshape(GRID, stride_rows, GRID, stride_cols, channels).transpose(1, 3, 0, 2, 4)
    group_total = stride_rows * stride_cols
    block = math.gcd(group_total, 8)
    grouped = grouped.reshape(group_total // block, block, GRID * GRID, channels)
    attended = lax.map(lambda part_groups: attend_groups(part_groups, attend_weight, output_weight), grouped)
    attended = attended.reshape(stride_rows, stride_cols, GRID, GRID, channels).transpose(2, 0, 3, 1, 4)
    attention = attended.reshape(height, width, channels)
    return (mbconv.astype(jnp.float32) + attention.astype(jnp.float32)).astype(jnp.bfloat16)
```

```python
import functools
import math

import jax
import jax.numpy as jnp
from jax import lax
from jax.experimental import pallas as pl
from jax.experimental.pallas import tpu as pltpu
from jax.sharding import PartitionSpec as P

HEADS = 16
HEAD_DIM = 32
GRID = 16
LANES = 128
MESH = pl.DeviceIdType.MESH


def gelu_tanh(values):
    half = 0.5 * values
    inner = values * (0.7978845608028654 + 0.035677408136300125 * (values * values))
    return half + half * jnp.tanh(inner)


def kernel(
    row_count,
    col_count,
    spread,
    blocks,
    row_order,
    x_ref,
    dk_ref,
    gain_ref,
    ew_hbm,
    pw_hbm,
    aw_hbm,
    ow_hbm,
    out_ref,
    ew,
    pw,
    aw,
    ow,
    hrows,
    ledge,
    redge,
    xe,
    expanded,
    depth,
    branch,
    mb,
    sendbuf,
    recvbuf,
    qkv,
    heads,
    backbuf,
    retbuf,
    weight_sem,
    halo_send,
    halo_recv,
    fwd_send,
    fwd_recv,
    back_send,
    back_recv,
):
    tile_rows, tile_tokens, channels = x_ref.shape
    hidden = ew.shape[1]
    kinds, per_kind, team, piece, _ = sendbuf.shape
    residues = tile_tokens // blocks
    group_count = piece // blocks
    row = lax.axis_index("row")
    col = lax.axis_index("col")
    total = row_count * col_count
    me = row * col_count + col
    own = (row // spread) * col_count + col

    def member(index):
        return {"row": (index // col_count) * spread + row % spread, "col": index % col_count}

    weights = [
        pltpu.make_async_copy(src, dst, weight_sem.at[i])
        for i, (src, dst) in enumerate(((ew_hbm, ew), (pw_hbm, pw), (aw_hbm, aw), (ow_hbm, ow)))
    ]
    for copy in weights:
        copy.start()

    barrier = pltpu.get_barrier_semaphore()

    def greet(step, carry):
        other = lax.rem(me + step, total)
        pl.semaphore_signal(
            barrier,
            inc=1,
            device_id={"row": other // col_count, "col": lax.rem(other, col_count)},
            device_id_type=MESH,
        )
        return carry

    lax.fori_loop(1, total, greet, 0)
    pl.semaphore_wait(barrier, total - 1)

    last = tile_rows - 1
    edge = ledge.shape[1]
    tail = pl.ds(tile_tokens - edge, edge)
    front = pl.ds(0, edge)
    up, down, left, right = row > 0, row < row_count - 1, col > 0, col < col_count - 1
    halos = [
        (right, left, 0, 1, x_ref.at[:, tail], ledge.at[pl.ds(1, tile_rows)]),
        (left, right, 0, -1, x_ref.at[:, front], redge.at[pl.ds(1, tile_rows)]),
        (down, up, 1, 0, x_ref.at[last], hrows.at[0]),
        (up, down, -1, 0, x_ref.at[0], hrows.at[1]),
        (down & right, up & left, 1, 1, x_ref.at[last, tail], ledge.at[0]),
        (up & right, down & left, -1, 1, x_ref.at[0, tail], ledge.at[tile_rows + 1]),
        (down & left, up & right, 1, -1, x_ref.at[last, front], redge.at[0]),
        (up & left, down & right, -1, -1, x_ref.at[0, front], redge.at[tile_rows + 1]),
    ]

    def halo_copy(i):
        _, _, dr, dc, src, dst = halos[i]
        return pltpu.make_async_remote_copy(
            src_ref=src,
            dst_ref=dst,
            send_sem=halo_send.at[i],
            recv_sem=halo_recv.at[i],
            device_id={"row": row + dr, "col": col + dc},
            device_id_type=MESH,
        )

    for i, (sends, receives, _, _, _, dst) in enumerate(halos):

        @pl.when(sends)
        def _():
            halo_copy(i).start()

        @pl.when(jnp.logical_not(receives))
        def _():
            dst[...] = jnp.zeros(dst.shape, dst.dtype)

    def await_halo(indices):
        for i in indices:

            @pl.when(halos[i][1])
            def _():
                halo_copy(i).wait_recv()

    def stage(slot, source, ext):
        place = lax.broadcasted_iota(jnp.int32, (blocks, channels), 0)
        after = source[pl.ds(tile_tokens - edge, edge), :].astype(jnp.float32)[edge - blocks :]
        before = source[pl.ds(0, edge), :].astype(jnp.float32)[:blocks]
        low = ledge[ext].astype(jnp.float32)[edge - 1 : edge]
        high = redge[ext].astype(jnp.float32)[0:1]
        low = jnp.where(place == 0, low, pltpu.roll(after, 1, 0))
        high = jnp.where(place == blocks - 1, high, pltpu.roll(before, blocks - 1, 0))
        xe[slot, pl.ds(0, tile_tokens), :] = source[...]
        xe[slot, pl.ds(tile_tokens, 2 * blocks), :] = jnp.concatenate([low, high], axis=0).astype(
            jnp.bfloat16
        )

    def expand(rows):
        for slot, ext in enumerate(rows):
            if ext == 0:
                stage(slot, hrows.at[0], ext)
            elif ext == tile_rows + 1:
                stage(slot, hrows.at[1], ext)
            else:
                stage(slot, x_ref.at[ext - 1], ext)
        width = 256

        def columns(n, carry):
            lanes = pl.ds(pl.multiple_of(n * width, width), width)
            for slot, ext in enumerate(rows):
                product = jnp.dot(xe[slot], ew[:, lanes], preferred_element_type=jnp.float32)
                product = gelu_tanh(product).reshape(residues + 2, blocks, width)
                expanded[ext, pl.ds(1, residues), :, lanes] = product[:residues]
                expanded[ext, 0, :, lanes] = product[residues]
                expanded[ext, residues + 1, :, lanes] = product[residues + 1]
            return carry

        lax.fori_loop(0, hidden // width, columns, 0)

    def mbconv_row(i):
        part = 8

        def channel(n, carry):
            lanes = pl.ds(pl.multiple_of(n * LANES, LANES), LANES)
            taps = [[dk_ref[dr, pl.ds(dc, 1), lanes] for dc in range(3)] for dr in range(3)]
            for start in range(0, residues, part):
                acc = None
                for dr in range(3):
                    window = expanded[i + dr, pl.ds(start, part + 2), :, lanes]
                    for dc in range(3):
                        term = window[dc : dc + part] * taps[dr][dc]
                        acc = term if acc is None else acc + term
                value = gelu_tanh(acc).reshape(part * blocks, LANES).astype(jnp.bfloat16)
                depth[pl.ds(start * blocks, part * blocks), lanes] = value
            return carry

        lax.fori_loop(0, hidden // LANES, channel, 0)
        width = 256

        def project(n, carry):
            lanes = pl.ds(pl.multiple_of(n * width, width), width)
            branch[:, lanes] = jnp.dot(depth[...], pw[:, lanes], preferred_element_type=jnp.float32)
            return carry

        lax.fori_loop(0, channels // width, project, 0)
        kind, step = i % kinds, i // kinds
        chunk = tile_tokens // 8

        def norm(n, carry):
            rows = pl.ds(pl.multiple_of(n * chunk, chunk), chunk)
            value = (x_ref[i, rows, :].astype(jnp.float32) + branch[rows, :]).astype(jnp.bfloat16)
            mb[i, rows, :] = value
            value = value.astype(jnp.float32)
            center = jnp.mean(value, axis=-1, keepdims=True)
            value = value - center
            scale = lax.rsqrt(jnp.mean(value * value, axis=-1, keepdims=True) + 1e-05)
            normed = (value * scale * gain_ref[...]).astype(jnp.bfloat16)
            count = chunk // piece
            sendbuf[kind, step, pl.ds(n * count, count)] = normed.reshape(count, piece, channels)
            return carry

        lax.fori_loop(0, tile_tokens // chunk, norm, 0)

        def send(n, carry):
            other = lax.rem(own + n, team)
            forward_copy(kind, step, other, own).start()
            return carry

        lax.fori_loop(1, team, send, 0)
        recvbuf[kind, step, own] = sendbuf[kind, step, own]

    def forward_copy(kind, step, other, slot):
        return pltpu.make_async_remote_copy(
            src_ref=sendbuf.at[kind, step, other],
            dst_ref=recvbuf.at[kind, step, slot],
            send_sem=fwd_send.at[kind, step, other],
            recv_sem=fwd_recv.at[kind, step, slot],
            device_id=member(other),
            device_id_type=MESH,
        )

    def back_copy(kind, other, slot):
        return pltpu.make_async_remote_copy(
            src_ref=backbuf.at[kind, :, other],
            dst_ref=retbuf.at[kind, :, slot],
            send_sem=back_send.at[kind, other],
            recv_sem=back_recv.at[kind, slot],
            device_id=member(other),
            device_id_type=MESH,
        )

    def attend(kind):
        def arrive(n, carry):
            other = lax.rem(own + n, team)
            for step in range(per_kind):
                forward_copy(kind, step, other, other).wait_recv()
            return carry

        lax.fori_loop(1, team, arrive, 0)
        members = per_kind * team * blocks
        scale = math.log2(math.e) / math.sqrt(HEAD_DIM)
        width = 256

        def projection(n, carry):
            lanes = pl.ds(pl.multiple_of(n * width, width), width)
            group_tokens = recvbuf[kind].reshape(per_kind * team * piece, channels)
            value = jnp.dot(group_tokens, aw[:, lanes], preferred_element_type=jnp.float32)
            value = value * jnp.where(n * width < channels, scale, 1.0)
            value = value.reshape(per_kind * team, piece, width)
            for g in range(group_count):
                one = value[:, g * blocks : (g + 1) * blocks].reshape(members, width)
                qkv[g, :, lanes] = one.astype(jnp.bfloat16)
            return carry

        lax.fori_loop(0, 3 * channels // width, projection, 0)
        per_block = LANES // HEAD_DIM
        head_of = lax.broadcasted_iota(jnp.int32, (members, LANES), 1) // HEAD_DIM
        ones = jnp.ones((members, LANES), jnp.bfloat16)
        for g in range(group_count):

            def head_block(n, carry):
                base = n * LANES
                lanes = pl.ds(pl.multiple_of(base, LANES), LANES)
                queries = qkv[g, :, lanes]
                keys = qkv[g, :, pl.ds(pl.multiple_of(base + channels, LANES), LANES)]
                values = qkv[g, :, pl.ds(pl.multiple_of(base + 2 * channels, LANES), LANES)]
                values = jnp.concatenate([values, ones], axis=1)
                result = jnp.zeros((members, LANES), jnp.float32)
                for h in range(per_block):
                    mask = (head_of == h).astype(jnp.float32).astype(jnp.bfloat16)
                    scores = lax.dot_general(
                        queries * mask,
                        keys,
                        (((1,), (1,)), ((), ())),
                        preferred_element_type=jnp.float32,
                    )
                    top = jnp.max(scores, axis=-1, keepdims=True)
                    soft = jnp.exp2(scores - top).astype(jnp.bfloat16)
                    both = jnp.dot(soft, values, preferred_element_type=jnp.float32)
                    result = jnp.where(head_of == h, both[:, :LANES] / both[:, LANES:], result)
                heads[:, pl.ds(g * blocks, blocks), lanes] = result.reshape(
                    per_kind * team, blocks, LANES
                )
                return carry

            lax.fori_loop(0, channels // LANES, head_block, 0)

        merged = heads[...].reshape(per_kind * team * piece, channels).astype(jnp.bfloat16)
        result = jnp.dot(merged, ow[...], preferred_element_type=jnp.float32)
        backbuf[kind] = result.astype(jnp.bfloat16).reshape(per_kind, team, piece, channels)

        def send(n, carry):
            back_copy(kind, lax.rem(own + n, team), own).start()
            return carry

        lax.fori_loop(1, team, send, 0)
        for step in range(per_kind):
            retbuf[kind, step, own] = backbuf[kind, step, own]

    def finish(kind):
        def arrive(n, carry):
            other = lax.rem(own + n, team)
            back_copy(kind, other, other).wait_recv()
            return carry

        lax.fori_loop(1, team, arrive, 0)
        for step in range(per_kind):
            i = step * kinds + kind
            attention = retbuf[kind, step].reshape(tile_tokens, channels).astype(jnp.float32)
            out_ref[i] = (mb[i].astype(jnp.float32) + attention).astype(jnp.bfloat16)

    weights[0].wait()
    await_halo((0, 1))
    expand([1, 2, 3])
    weights[1].wait()
    mbconv_row(row_order[0])
    await_halo(range(2, len(halos)))
    expand([*range(4, tile_rows + 2), 0])
    for i in row_order[1:]:
        mbconv_row(i)
    weights[2].wait()
    weights[3].wait()
    kind_order = list(dict.fromkeys(i % kinds for i in row_order))
    for kind in kind_order:
        attend(kind)
    for kind in kind_order:
        finish(kind)

    for i, (sends, *_) in enumerate(halos):

        @pl.when(sends)
        def _():
            halo_copy(i).wait_send()

    def drain(n, carry):
        other = lax.rem(own + n, team)
        for kind in range(kinds):
            for step in range(per_kind):
                forward_copy(kind, step, other, own).wait_send()
            back_copy(kind, other, own).wait_send()
        return carry

    lax.fori_loop(1, team, drain, 0)


def local(
    tokens, expand_weight, depth_kernel, project_weight, norm_gain, attend_weight, output_weight
):
    tile_rows, tile_cols, channels = tokens.shape
    hidden = expand_weight.shape[1]
    row_count = lax.axis_size("row")
    col_count = lax.axis_size("col")
    stride_rows = tile_rows * row_count // GRID
    stride_cols = tile_cols * col_count // GRID
    blocks = tile_cols // stride_cols
    spread = max(1, stride_rows // tile_rows)
    kinds = min(stride_rows, tile_rows)
    per_kind = tile_rows // kinds
    team = row_count // spread * col_count
    piece = stride_cols // team * blocks
    row_order = [i for i in range(1, tile_rows) if i % kinds == 1 % kinds]
    row_order += [i for i in range(tile_rows - 1, -1, -1) if i not in row_order]
    ordered = tokens.reshape(tile_rows, blocks, stride_cols, channels).transpose(0, 2, 1, 3)
    ordered = ordered.reshape(tile_rows, tile_cols, channels)
    bf16, f32 = jnp.bfloat16, jnp.float32
    exchange = (kinds, per_kind, team, piece, channels)
    out = pl.pallas_call(
        functools.partial(kernel, row_count, col_count, spread, blocks, row_order),
        out_shape=jax.ShapeDtypeStruct((tile_rows, tile_cols, channels), bf16),
        in_specs=[pl.BlockSpec(memory_space=pltpu.VMEM)] * 3
        + [pl.BlockSpec(memory_space=pl.ANY)] * 4,
        out_specs=pl.BlockSpec(memory_space=pltpu.VMEM),
        scratch_shapes=[
            pltpu.VMEM(expand_weight.shape, bf16),
            pltpu.VMEM(project_weight.shape, bf16),
            pltpu.VMEM(attend_weight.shape, bf16),
            pltpu.VMEM(output_weight.shape, bf16),
            pltpu.VMEM((2, tile_cols, channels), bf16),
            pltpu.VMEM((tile_rows + 2, 16, channels), bf16),
            pltpu.VMEM((tile_rows + 2, 16, channels), bf16),
            pltpu.VMEM((3, tile_cols + 2 * blocks, channels), bf16),
            pltpu.VMEM((tile_rows + 2, stride_cols + 2, blocks, hidden), f32),
            pltpu.VMEM((tile_cols, hidden), bf16),
            pltpu.VMEM((tile_cols, channels), f32),
            pltpu.VMEM((tile_rows, tile_cols, channels), bf16),
            pltpu.VMEM(exchange, bf16),
            pltpu.VMEM(exchange, bf16),
            pltpu.VMEM((piece // blocks, per_kind * team * blocks, 3 * channels), bf16),
            pltpu.VMEM((per_kind * team, piece, channels), f32),
            pltpu.VMEM(exchange, bf16),
            pltpu.VMEM(exchange, bf16),
            pltpu.SemaphoreType.DMA((4,)),
            pltpu.SemaphoreType.DMA((8,)),
            pltpu.SemaphoreType.DMA((8,)),
            pltpu.SemaphoreType.DMA((kinds, per_kind, team)),
            pltpu.SemaphoreType.DMA((kinds, per_kind, team)),
            pltpu.SemaphoreType.DMA((kinds, team)),
            pltpu.SemaphoreType.DMA((kinds, team)),
        ],
        compiler_params=pltpu.CompilerParams(
            collective_id=0, has_side_effects=True, vmem_limit_bytes=52 * 1024 * 1024
        ),
    )(
        ordered,
        depth_kernel,
        norm_gain.reshape(1, channels),
        expand_weight,
        project_weight,
        attend_weight,
        output_weight,
    )
    out = out.reshape(tile_rows, stride_cols, blocks, channels).transpose(0, 2, 1, 3)
    return out.reshape(tile_rows, tile_cols, channels)


def solution(mesh):
    placed = (P(("parts", "row"), "col", None), P(), P(), P(), P(), P(), P())
    return jax.shard_map(
        local,
        mesh=mesh,
        in_specs=placed,
        out_specs=P(("parts", "row"), "col", None),
        check_vma=False,
    )
```

```python
import functools
import math

import jax
import jax.numpy as jnp
from jax import lax
from jax.experimental import pallas as pl
from jax.experimental.pallas import tpu as pltpu
from jax.sharding import PartitionSpec as P

HEADS = 16
HEAD_DIM = 32
GRID = 16
LANES = 128
MESH = pl.DeviceIdType.MESH


def gelu_of_double(half):
    inner = half * (1.5957691216057308 + 0.285419265090401 * (half * half))
    return half + half * jnp.tanh(inner)


def kernel(
    row_count,
    col_count,
    spread,
    blocks,
    row_order,
    x_ref,
    dk_ref,
    gain_ref,
    ew_hbm,
    pw_hbm,
    aw_hbm,
    ow_hbm,
    out_ref,
    ew,
    pw,
    aw,
    ow,
    hrows,
    ledge,
    redge,
    perm,
    xe,
    expanded,
    depth,
    branch,
    mb,
    sendbuf,
    recvbuf,
    qkv,
    heads,
    backbuf,
    retbuf,
    weight_sem,
    halo_send,
    halo_recv,
    fwd_send,
    fwd_recv,
    back_send,
    back_recv,
):
    tile_rows, tile_tokens, channels = x_ref.shape
    hidden = ew.shape[1]
    kinds, per_kind, team, piece, _ = sendbuf.shape
    residues = tile_tokens // blocks
    group_count = piece // blocks
    row = lax.axis_index("row")
    col = lax.axis_index("col")
    total = row_count * col_count
    me = row * col_count + col
    own = (row // spread) * col_count + col

    def member(index):
        return {"row": (index // col_count) * spread + row % spread, "col": index % col_count}

    weights = [
        pltpu.make_async_copy(src, dst, weight_sem.at[i])
        for i, (src, dst) in enumerate(((ew_hbm, ew), (pw_hbm, pw), (aw_hbm, aw), (ow_hbm, ow)))
    ]
    for copy in weights:
        copy.start()

    barrier = pltpu.get_barrier_semaphore()

    def greet(step, carry):
        other = lax.rem(me + step, total)
        pl.semaphore_signal(
            barrier,
            inc=1,
            device_id={"row": other // col_count, "col": lax.rem(other, col_count)},
            device_id_type=MESH,
        )
        return carry

    lax.fori_loop(1, total, greet, 0)

    target = lax.broadcasted_iota(jnp.int32, perm.shape, 0)
    origin = lax.broadcasted_iota(jnp.int32, perm.shape, 1)
    residue = target // blocks
    chosen = origin == (target - residue * blocks) * residues + residue
    perm[...] = jnp.where(chosen, 0.5, 0.0).astype(jnp.bfloat16)

    def permute(ext, source):
        value = jnp.dot(perm[...], source[...], preferred_element_type=jnp.float32)
        xe[ext, pl.ds(0, tile_tokens), :] = value.astype(jnp.bfloat16)

    for ext in range(1, 4):
        permute(ext, x_ref.at[ext - 1])

    pl.semaphore_wait(barrier, total - 1)

    last = tile_rows - 1
    edge = ledge.shape[1]
    tail = pl.ds(tile_tokens - edge, edge)
    front = pl.ds(0, edge)
    up, down, left, right = row > 0, row < row_count - 1, col > 0, col < col_count - 1
    halos = [
        (right, left, 0, 1, x_ref.at[:, tail], ledge.at[pl.ds(1, tile_rows)]),
        (left, right, 0, -1, x_ref.at[:, front], redge.at[pl.ds(1, tile_rows)]),
        (down, up, 1, 0, x_ref.at[last], hrows.at[0]),
        (up, down, -1, 0, x_ref.at[0], hrows.at[1]),
        (down & right, up & left, 1, 1, x_ref.at[last, tail], ledge.at[0]),
        (up & right, down & left, -1, 1, x_ref.at[0, tail], ledge.at[tile_rows + 1]),
        (down & left, up & right, 1, -1, x_ref.at[last, front], redge.at[0]),
        (up & left, down & right, -1, -1, x_ref.at[0, front], redge.at[tile_rows + 1]),
    ]

    def halo_copy(i):
        _, _, dr, dc, src, dst = halos[i]
        return pltpu.make_async_remote_copy(
            src_ref=src,
            dst_ref=dst,
            send_sem=halo_send.at[i],
            recv_sem=halo_recv.at[i],
            device_id={"row": row + dr, "col": col + dc},
            device_id_type=MESH,
        )

    for i, (sends, receives, _, _, _, dst) in enumerate(halos):

        @pl.when(sends)
        def _():
            halo_copy(i).start()

        @pl.when(jnp.logical_not(receives))
        def _():
            dst[...] = jnp.zeros(dst.shape, dst.dtype)

    def await_halo(indices):
        for i in indices:

            @pl.when(halos[i][1])
            def _():
                halo_copy(i).wait_recv()

    def border(ext):
        place = lax.broadcasted_iota(jnp.int32, (blocks, channels), 0)
        after = xe[ext, pl.ds(tile_tokens - edge, edge), :].astype(jnp.float32)[edge - blocks :]
        before = xe[ext, pl.ds(0, edge), :].astype(jnp.float32)[:blocks]
        low = 0.5 * ledge[ext].astype(jnp.float32)[edge - 1 : edge]
        high = 0.5 * redge[ext].astype(jnp.float32)[0:1]
        low = jnp.where(place == 0, low, pltpu.roll(after, 1, 0))
        high = jnp.where(place == blocks - 1, high, pltpu.roll(before, blocks - 1, 0))
        xe[ext, pl.ds(tile_tokens, 2 * blocks), :] = jnp.concatenate([low, high], axis=0).astype(
            jnp.bfloat16
        )

    def expand(rows):
        for ext in rows:
            border(ext)
        width = 256

        def columns(n, carry):
            lanes = pl.ds(pl.multiple_of(n * width, width), width)
            for ext in rows:
                product = jnp.dot(xe[ext], ew[:, lanes], preferred_element_type=jnp.float32)
                product = gelu_of_double(product).reshape(residues + 2, blocks, width)
                expanded[ext, pl.ds(1, residues), :, lanes] = product[:residues]
                expanded[ext, 0, :, lanes] = product[residues]
                expanded[ext, residues + 1, :, lanes] = product[residues + 1]
            return carry

        lax.fori_loop(0, hidden // width, columns, 0)

    def mbconv_row(i):
        part = 8

        def channel(n, carry):
            lanes = pl.ds(pl.multiple_of(n * LANES, LANES), LANES)
            taps = [[0.5 * dk_ref[dr, pl.ds(dc, 1), lanes] for dc in range(3)] for dr in range(3)]
            for start in range(0, residues, part):
                acc = None
                for dr in range(3):
                    window = expanded[i + dr, pl.ds(start, part + 2), :, lanes]
                    for dc in range(3):
                        term = window[dc : dc + part] * taps[dr][dc]
                        acc = term if acc is None else acc + term
                value = gelu_of_double(acc).reshape(part * blocks, LANES).astype(jnp.bfloat16)
                depth[pl.ds(start * blocks, part * blocks), lanes] = value
            return carry

        lax.fori_loop(0, hidden // LANES, channel, 0)
        width = 256

        def project(n, carry):
            lanes = pl.ds(pl.multiple_of(n * width, width), width)
            branch[:, lanes] = jnp.dot(depth[...], pw[:, lanes], preferred_element_type=jnp.float32)
            return carry

        lax.fori_loop(0, channels // width, project, 0)
        kind, step = i % kinds, i // kinds
        chunk = tile_tokens // 8
        count = chunk // piece
        for n in range(tile_tokens // chunk):
            rows = pl.ds(n * chunk, chunk)
            value = 2.0 * xe[i + 1, rows, :].astype(jnp.float32) + branch[rows, :]
            value = value.astype(jnp.bfloat16)
            mb[i, rows, :] = value
            value = value.astype(jnp.float32)
            center = jnp.mean(value, axis=-1, keepdims=True)
            value = value - center
            scale = lax.rsqrt(jnp.mean(value * value, axis=-1, keepdims=True) + 1e-05)
            normed = (value * scale * gain_ref[...]).astype(jnp.bfloat16)
            sendbuf[kind, step, pl.ds(n * count, count)] = normed.reshape(count, piece, channels)

        def send(n, carry):
            other = lax.rem(own + n, team)
            forward_copy(kind, step, other, own).start()
            return carry

        lax.fori_loop(1, team, send, 0)
        recvbuf[kind, step, own] = sendbuf[kind, step, own]

    def forward_copy(kind, step, other, slot):
        return pltpu.make_async_remote_copy(
            src_ref=sendbuf.at[kind, step, other],
            dst_ref=recvbuf.at[kind, step, slot],
            send_sem=fwd_send.at[kind, step, other],
            recv_sem=fwd_recv.at[kind, step, slot],
            device_id=member(other),
            device_id_type=MESH,
        )

    def back_copy(kind, group, other, slot):
        return pltpu.make_async_remote_copy(
            src_ref=backbuf.at[kind, group, other],
            dst_ref=retbuf.at[kind, group, slot],
            send_sem=back_send.at[kind, group, other],
            recv_sem=back_recv.at[kind, group, slot],
            device_id=member(other),
            device_id_type=MESH,
        )

    def attend(kind):
        def arrive(n, carry):
            other = lax.rem(own + n, team)
            for step in range(per_kind):
                forward_copy(kind, step, other, other).wait_recv()
            return carry

        lax.fori_loop(1, team, arrive, 0)
        members = per_kind * team * blocks
        scale = math.log2(math.e) / math.sqrt(HEAD_DIM)
        width = 256

        def projection(n, carry):
            lanes = pl.ds(pl.multiple_of(n * width, width), width)
            group_tokens = recvbuf[kind].reshape(per_kind * team * piece, channels)
            value = jnp.dot(group_tokens, aw[:, lanes], preferred_element_type=jnp.float32)
            value = value * jnp.where(n * width < channels, scale, 1.0)
            value = value.reshape(per_kind * team, piece, width)
            for g in range(group_count):
                one = value[:, g * blocks : (g + 1) * blocks].reshape(members, width)
                qkv[g, :, lanes] = one.astype(jnp.bfloat16)
            return carry

        lax.fori_loop(0, 3 * channels // width, projection, 0)
        per_block = LANES // HEAD_DIM
        head_of = lax.broadcasted_iota(jnp.int32, (members, LANES), 1) // HEAD_DIM
        ones = jnp.ones((members, LANES), jnp.bfloat16)
        masks = [(head_of == h).astype(jnp.float32).astype(jnp.bfloat16) for h in range(per_block)]
        for g in range(group_count):

            def head_block(n, carry):
                base = n * LANES
                lanes = pl.ds(pl.multiple_of(base, LANES), LANES)
                queries = qkv[g, :, lanes]
                keys = qkv[g, :, pl.ds(pl.multiple_of(base + channels, LANES), LANES)]
                values = qkv[g, :, pl.ds(pl.multiple_of(base + 2 * channels, LANES), LANES)]
                values = jnp.concatenate([values, ones], axis=1)
                stacked = jnp.concatenate([queries * mask for mask in masks], axis=0)
                scores = lax.dot_general(
                    stacked, keys, (((1,), (1,)), ((), ())), preferred_element_type=jnp.float32
                )
                top = jnp.max(scores, axis=-1, keepdims=True)
                soft = jnp.exp2(scores - top).astype(jnp.bfloat16)
                both = jnp.dot(soft, values, preferred_element_type=jnp.float32)
                both = both.reshape(per_block, members, 2 * LANES)
                above, below = both[0, :, :LANES], both[0, :, LANES:]
                for h in range(1, per_block):
                    above = jnp.where(head_of == h, both[h, :, :LANES], above)
                    below = jnp.where(head_of == h, both[h, :, LANES:], below)
                heads[:, lanes] = (above / below).astype(jnp.bfloat16)
                return carry

            lax.fori_loop(0, channels // LANES, head_block, 0)
            result = jnp.dot(heads[...], ow[...], preferred_element_type=jnp.float32)
            result = result.reshape(per_kind, team, blocks, channels)
            result = jnp.concatenate([result[step] for step in range(per_kind)], axis=1)
            backbuf[kind, g] = result.astype(jnp.bfloat16)

            def send(n, carry):
                back_copy(kind, g, lax.rem(own + n, team), own).start()
                return carry

            lax.fori_loop(1, team, send, 0)
            retbuf[kind, g, own] = backbuf[kind, g, own]

    def finish(kind):
        def arrive(n, carry):
            other = lax.rem(own + n, team)
            for g in range(group_count):
                back_copy(kind, g, other, other).wait_recv()
            return carry

        lax.fori_loop(1, team, arrive, 0)
        for step in range(per_kind):
            i = step * kinds + kind
            attention = [
                retbuf[kind, g].astype(jnp.float32)[:, step * blocks : (step + 1) * blocks]
                for g in range(group_count)
            ]
            attention = jnp.concatenate(attention, axis=1).reshape(tile_tokens, channels)
            out_ref[i] = (mb[i].astype(jnp.float32) + attention).astype(jnp.bfloat16)

    weights[0].wait()
    await_halo((0, 1))
    expand([1, 2, 3])
    weights[1].wait()
    mbconv_row(row_order[0])
    await_halo(range(2, len(halos)))
    permute(0, hrows.at[0])
    permute(tile_rows + 1, hrows.at[1])
    for ext in range(4, tile_rows + 1):
        permute(ext, x_ref.at[ext - 1])
    expand([*range(4, tile_rows + 2), 0])
    for i in row_order[1:]:
        mbconv_row(i)
    weights[2].wait()
    weights[3].wait()
    kind_order = list(dict.fromkeys(i % kinds for i in row_order))
    for kind in kind_order:
        attend(kind)
    for kind in kind_order:
        finish(kind)

    for i, (sends, *_) in enumerate(halos):

        @pl.when(sends)
        def _():
            halo_copy(i).wait_send()

    def drain(n, carry):
        other = lax.rem(own + n, team)
        for kind in range(kinds):
            for step in range(per_kind):
                forward_copy(kind, step, other, own).wait_send()
            for g in range(group_count):
                back_copy(kind, g, other, own).wait_send()
        return carry

    lax.fori_loop(1, team, drain, 0)


def local(
    tokens, expand_weight, depth_kernel, project_weight, norm_gain, attend_weight, output_weight
):
    tile_rows, tile_cols, channels = tokens.shape
    hidden = expand_weight.shape[1]
    row_count = lax.axis_size("row")
    col_count = lax.axis_size("col")
    stride_rows = tile_rows * row_count // GRID
    stride_cols = tile_cols * col_count // GRID
    blocks = tile_cols // stride_cols
    spread = max(1, stride_rows // tile_rows)
    kinds = min(stride_rows, tile_rows)
    per_kind = tile_rows // kinds
    team = row_count // spread * col_count
    piece = stride_cols // team * blocks
    row_order = [i for i in range(1, tile_rows) if i % kinds == 1 % kinds]
    row_order += [i for i in range(tile_rows - 1, -1, -1) if i not in row_order]
    bf16, f32 = jnp.bfloat16, jnp.float32
    exchange = (kinds, per_kind, team, piece, channels)
    returned = (kinds, piece // blocks, team, per_kind * blocks, channels)
    out = pl.pallas_call(
        functools.partial(kernel, row_count, col_count, spread, blocks, row_order),
        out_shape=jax.ShapeDtypeStruct((tile_rows, tile_cols, channels), bf16),
        in_specs=[pl.BlockSpec(memory_space=pltpu.VMEM)] * 3
        + [pl.BlockSpec(memory_space=pl.ANY)] * 4,
        out_specs=pl.BlockSpec(memory_space=pltpu.VMEM),
        scratch_shapes=[
            pltpu.VMEM(expand_weight.shape, bf16),
            pltpu.VMEM(project_weight.shape, bf16),
            pltpu.VMEM(attend_weight.shape, bf16),
            pltpu.VMEM(output_weight.shape, bf16),
            pltpu.VMEM((2, tile_cols, channels), bf16),
            pltpu.VMEM((tile_rows + 2, 16, channels), bf16),
            pltpu.VMEM((tile_rows + 2, 16, channels), bf16),
            pltpu.VMEM((tile_cols, tile_cols), bf16),
            pltpu.VMEM((tile_rows + 2, tile_cols + 2 * blocks, channels), bf16),
            pltpu.VMEM((tile_rows + 2, stride_cols + 2, blocks, hidden), f32),
            pltpu.VMEM((tile_cols, hidden), bf16),
            pltpu.VMEM((tile_cols, channels), f32),
            pltpu.VMEM((tile_rows, tile_cols, channels), bf16),
            pltpu.VMEM(exchange, bf16),
            pltpu.VMEM(exchange, bf16),
            pltpu.VMEM((piece // blocks, per_kind * team * blocks, 3 * channels), bf16),
            pltpu.VMEM((per_kind * team * blocks, channels), bf16),
            pltpu.VMEM(returned, bf16),
            pltpu.VMEM(returned, bf16),
            pltpu.SemaphoreType.DMA((4,)),
            pltpu.SemaphoreType.DMA((8,)),
            pltpu.SemaphoreType.DMA((8,)),
            pltpu.SemaphoreType.DMA((kinds, per_kind, team)),
            pltpu.SemaphoreType.DMA((kinds, per_kind, team)),
            pltpu.SemaphoreType.DMA((kinds, piece // blocks, team)),
            pltpu.SemaphoreType.DMA((kinds, piece // blocks, team)),
        ],
        compiler_params=pltpu.CompilerParams(
            collective_id=0, has_side_effects=True, vmem_limit_bytes=52 * 1024 * 1024
        ),
    )(
        tokens,
        depth_kernel,
        norm_gain.reshape(1, channels),
        expand_weight,
        project_weight,
        attend_weight,
        output_weight,
    )
    out = out.reshape(tile_rows, stride_cols, blocks, channels).transpose(0, 2, 1, 3)
    return out.reshape(tile_rows, tile_cols, channels)


def solution(mesh):
    placed = (P(("parts", "row"), "col", None), P(), P(), P(), P(), P(), P())
    return jax.shard_map(
        local,
        mesh=mesh,
        in_specs=placed,
        out_specs=P(("parts", "row"), "col", None),
        check_vma=False,
    )
```

```python
import functools
import math

import jax
import jax.numpy as jnp
from jax import lax
from jax.experimental import pallas as pl
from jax.experimental.pallas import tpu as pltpu
from jax.sharding import PartitionSpec as P

HEADS = 16
HEAD_DIM = 32
GRID = 16
LANES = 128
MESH = pl.DeviceIdType.MESH


def gelu_of_double(half):
    inner = half * (1.5957691216057308 + 0.285419265090401 * (half * half))
    return half + half * jnp.tanh(inner)


def kernel(
    row_count,
    col_count,
    spread,
    blocks,
    row_order,
    x_ref,
    dk_ref,
    gain_ref,
    ew_hbm,
    pw_hbm,
    aw_hbm,
    ow_hbm,
    out_ref,
    ew,
    pw,
    aw,
    ow,
    hrows,
    ledge,
    redge,
    perm,
    xe,
    expanded,
    depth,
    branch,
    mb,
    sendbuf,
    recvbuf,
    queries_t,
    keys,
    values_t,
    heads_t,
    backbuf,
    retbuf,
    weight_sem,
    halo_send,
    halo_recv,
    fwd_send,
    fwd_recv,
    back_send,
    back_recv,
):
    tile_rows, tile_tokens, channels = x_ref.shape
    hidden = ew.shape[1]
    kinds, per_kind, team, piece, _ = sendbuf.shape
    residues = tile_tokens // blocks
    group_count = piece // blocks
    row = lax.axis_index("row")
    col = lax.axis_index("col")
    total = row_count * col_count
    me = row * col_count + col
    own = (row // spread) * col_count + col

    def member(index):
        return {"row": (index // col_count) * spread + row % spread, "col": index % col_count}

    weights = [
        pltpu.make_async_copy(src, dst, weight_sem.at[i])
        for i, (src, dst) in enumerate(((ew_hbm, ew), (pw_hbm, pw), (aw_hbm, aw), (ow_hbm, ow)))
    ]
    for copy in weights:
        copy.start()

    barrier = pltpu.get_barrier_semaphore()

    def greet(step, carry):
        other = lax.rem(me + step, total)
        pl.semaphore_signal(
            barrier,
            inc=1,
            device_id={"row": other // col_count, "col": lax.rem(other, col_count)},
            device_id_type=MESH,
        )
        return carry

    lax.fori_loop(1, total, greet, 0)

    target = lax.broadcasted_iota(jnp.int32, perm.shape, 0)
    origin = lax.broadcasted_iota(jnp.int32, perm.shape, 1)
    residue = target // blocks
    chosen = origin == (target - residue * blocks) * residues + residue
    perm[...] = jnp.where(chosen, 0.5, 0.0).astype(jnp.bfloat16)

    def permute(ext, source):
        value = jnp.dot(perm[...], source[...], preferred_element_type=jnp.float32)
        xe[ext, pl.ds(0, tile_tokens), :] = value.astype(jnp.bfloat16)

    for ext in range(1, 4):
        permute(ext, x_ref.at[ext - 1])

    pl.semaphore_wait(barrier, total - 1)

    last = tile_rows - 1
    edge = ledge.shape[1]
    tail = pl.ds(tile_tokens - edge, edge)
    front = pl.ds(0, edge)
    up, down, left, right = row > 0, row < row_count - 1, col > 0, col < col_count - 1
    halos = [
        (right, left, 0, 1, x_ref.at[:, tail], ledge.at[pl.ds(1, tile_rows)]),
        (left, right, 0, -1, x_ref.at[:, front], redge.at[pl.ds(1, tile_rows)]),
        (down, up, 1, 0, x_ref.at[last], hrows.at[0]),
        (up, down, -1, 0, x_ref.at[0], hrows.at[1]),
        (down & right, up & left, 1, 1, x_ref.at[last, tail], ledge.at[0]),
        (up & right, down & left, -1, 1, x_ref.at[0, tail], ledge.at[tile_rows + 1]),
        (down & left, up & right, 1, -1, x_ref.at[last, front], redge.at[0]),
        (up & left, down & right, -1, -1, x_ref.at[0, front], redge.at[tile_rows + 1]),
    ]

    def halo_copy(i):
        _, _, dr, dc, src, dst = halos[i]
        return pltpu.make_async_remote_copy(
            src_ref=src,
            dst_ref=dst,
            send_sem=halo_send.at[i],
            recv_sem=halo_recv.at[i],
            device_id={"row": row + dr, "col": col + dc},
            device_id_type=MESH,
        )

    for i, (sends, receives, _, _, _, dst) in enumerate(halos):

        @pl.when(sends)
        def _():
            halo_copy(i).start()

        @pl.when(jnp.logical_not(receives))
        def _():
            dst[...] = jnp.zeros(dst.shape, dst.dtype)

    def await_halo(indices):
        for i in indices:

            @pl.when(halos[i][1])
            def _():
                halo_copy(i).wait_recv()

    def border(ext):
        place = lax.broadcasted_iota(jnp.int32, (blocks, channels), 0)
        after = xe[ext, pl.ds(tile_tokens - edge, edge), :].astype(jnp.float32)[edge - blocks :]
        before = xe[ext, pl.ds(0, edge), :].astype(jnp.float32)[:blocks]
        low = 0.5 * ledge[ext].astype(jnp.float32)[edge - 1 : edge]
        high = 0.5 * redge[ext].astype(jnp.float32)[0:1]
        low = jnp.where(place == 0, low, pltpu.roll(after, 1, 0))
        high = jnp.where(place == blocks - 1, high, pltpu.roll(before, blocks - 1, 0))
        xe[ext, pl.ds(tile_tokens, 2 * blocks), :] = jnp.concatenate([low, high], axis=0).astype(
            jnp.bfloat16
        )

    def expand(rows):
        for ext in rows:
            border(ext)
        width = 256

        def columns(n, carry):
            lanes = pl.ds(pl.multiple_of(n * width, width), width)
            for ext in rows:
                product = jnp.dot(xe[ext], ew[:, lanes], preferred_element_type=jnp.float32)
                product = gelu_of_double(product).reshape(residues + 2, blocks, width)
                expanded[ext, pl.ds(1, residues), :, lanes] = product[:residues]
                expanded[ext, 0, :, lanes] = product[residues]
                expanded[ext, residues + 1, :, lanes] = product[residues + 1]
            return carry

        lax.fori_loop(0, hidden // width, columns, 0)

    def mbconv_row(i):
        part = 8

        def channel(n, carry):
            lanes = pl.ds(pl.multiple_of(n * LANES, LANES), LANES)
            taps = [[0.5 * dk_ref[dr, pl.ds(dc, 1), lanes] for dc in range(3)] for dr in range(3)]
            for start in range(0, residues, part):
                acc = None
                for dr in range(3):
                    window = expanded[i + dr, pl.ds(start, part + 2), :, lanes]
                    for dc in range(3):
                        term = window[dc : dc + part] * taps[dr][dc]
                        acc = term if acc is None else acc + term
                value = gelu_of_double(acc).reshape(part * blocks, LANES).astype(jnp.bfloat16)
                depth[pl.ds(start * blocks, part * blocks), lanes] = value
            return carry

        lax.fori_loop(0, hidden // LANES, channel, 0)
        width = 256

        def project(n, carry):
            lanes = pl.ds(pl.multiple_of(n * width, width), width)
            branch[:, lanes] = jnp.dot(depth[...], pw[:, lanes], preferred_element_type=jnp.float32)
            return carry

        lax.fori_loop(0, channels // width, project, 0)
        kind, step = i % kinds, i // kinds
        chunk = tile_tokens // 8
        count = chunk // piece
        for n in range(tile_tokens // chunk):
            rows = pl.ds(n * chunk, chunk)
            value = 2.0 * xe[i + 1, rows, :].astype(jnp.float32) + branch[rows, :]
            value = value.astype(jnp.bfloat16)
            mb[i, rows, :] = value
            value = value.astype(jnp.float32)
            center = jnp.mean(value, axis=-1, keepdims=True)
            value = value - center
            scale = lax.rsqrt(jnp.mean(value * value, axis=-1, keepdims=True) + 1e-05)
            normed = (value * scale * gain_ref[...]).astype(jnp.bfloat16)
            sendbuf[kind, step, pl.ds(n * count, count)] = normed.reshape(count, piece, channels)

        def send(n, carry):
            other = lax.rem(own + n, team)
            forward_copy(kind, step, other, own).start()
            return carry

        lax.fori_loop(1, team, send, 0)
        recvbuf[kind, step, own] = sendbuf[kind, step, own]

    def forward_copy(kind, step, other, slot):
        return pltpu.make_async_remote_copy(
            src_ref=sendbuf.at[kind, step, other],
            dst_ref=recvbuf.at[kind, step, slot],
            send_sem=fwd_send.at[kind, step, other],
            recv_sem=fwd_recv.at[kind, step, slot],
            device_id=member(other),
            device_id_type=MESH,
        )

    def back_copy(kind, group, other, slot):
        return pltpu.make_async_remote_copy(
            src_ref=backbuf.at[kind, group, other],
            dst_ref=retbuf.at[kind, group, slot],
            send_sem=back_send.at[kind, group, other],
            recv_sem=back_recv.at[kind, group, slot],
            device_id=member(other),
            device_id_type=MESH,
        )

    def attend(kind):
        def arrive(n, carry):
            other = lax.rem(own + n, team)
            for step in range(per_kind):
                forward_copy(kind, step, other, other).wait_recv()
            return carry

        lax.fori_loop(1, team, arrive, 0)
        members = per_kind * team * blocks
        scale = math.log2(math.e) / math.sqrt(HEAD_DIM)
        width = 256

        def projection(n, carry):
            for part in range(3):
                column = pl.multiple_of(part * channels + n * width, width)
                place = pl.ds(pl.multiple_of(n * width, width), width)
                group_tokens = recvbuf[kind].reshape(per_kind * team * piece, channels)
                value = jnp.dot(
                    group_tokens, aw[:, pl.ds(column, width)], preferred_element_type=jnp.float32
                )
                if part == 0:
                    value = value * scale
                value = value.reshape(per_kind * team, piece, width)
                for g in range(group_count):
                    one = value[:, g * blocks : (g + 1) * blocks].reshape(members, width)
                    if part == 1:
                        keys[g, :, place] = one.astype(jnp.bfloat16)
                    else:
                        store = queries_t if part == 0 else values_t
                        store[g, place, :] = one.T.astype(jnp.bfloat16)
            return carry

        lax.fori_loop(0, channels // width, projection, 0)
        per_block = LANES // HEAD_DIM
        unrolled = 2
        ones = jnp.ones((16, members), jnp.bfloat16)
        zeros = jnp.zeros((HEAD_DIM, members), jnp.bfloat16)
        for g in range(group_count):

            def head_block(n, carry):
                for m in range(unrolled):
                    base = pl.multiple_of((n * unrolled + m) * LANES, LANES)
                    key_block = keys[g, :, pl.ds(base, LANES)]
                    query_block = queries_t[g, pl.ds(base, LANES), :]
                    value_block = values_t[g, pl.ds(base, LANES), :]
                    for h in range(per_block):
                        rows = slice(h * HEAD_DIM, (h + 1) * HEAD_DIM)
                        query = [query_block[rows] if k == h else zeros for k in range(per_block)]
                        scores = jnp.dot(
                            key_block,
                            jnp.concatenate(query, axis=0),
                            preferred_element_type=jnp.float32,
                        )
                        top = jnp.max(scores, axis=0, keepdims=True)
                        soft = jnp.exp2(scores - top).astype(jnp.bfloat16)
                        both = jnp.dot(
                            jnp.concatenate([value_block[rows], ones], axis=0),
                            soft,
                            preferred_element_type=jnp.float32,
                        )
                        heads_t[pl.ds(base + h * HEAD_DIM, HEAD_DIM), :] = both[:HEAD_DIM] * (
                            1.0 / both[HEAD_DIM : HEAD_DIM + 1]
                        )
                return carry

            lax.fori_loop(0, channels // LANES // unrolled, head_block, 0)
            merged = heads_t[...].T.astype(jnp.bfloat16)
            result = jnp.dot(merged, ow[...], preferred_element_type=jnp.float32)
            result = result.reshape(per_kind, team, blocks, channels)
            result = jnp.concatenate([result[step] for step in range(per_kind)], axis=1)
            backbuf[kind, g] = result.astype(jnp.bfloat16)

            def send(n, carry):
                back_copy(kind, g, lax.rem(own + n, team), own).start()
                return carry

            lax.fori_loop(1, team, send, 0)
            retbuf[kind, g, own] = backbuf[kind, g, own]

    def finish(kind):
        def arrive(n, carry):
            other = lax.rem(own + n, team)
            for g in range(group_count):
                back_copy(kind, g, other, other).wait_recv()
            return carry

        lax.fori_loop(1, team, arrive, 0)
        for step in range(per_kind):
            i = step * kinds + kind
            attention = [
                retbuf[kind, g].astype(jnp.float32)[:, step * blocks : (step + 1) * blocks]
                for g in range(group_count)
            ]
            attention = jnp.concatenate(attention, axis=1).reshape(tile_tokens, channels)
            out_ref[i] = (mb[i].astype(jnp.float32) + attention).astype(jnp.bfloat16)

    weights[0].wait()
    await_halo((0, 1))
    expand([1, 2, 3])
    weights[1].wait()
    mbconv_row(row_order[0])
    await_halo(range(2, len(halos)))
    permute(0, hrows.at[0])
    permute(tile_rows + 1, hrows.at[1])
    for ext in range(4, tile_rows + 1):
        permute(ext, x_ref.at[ext - 1])
    expand([*range(4, tile_rows + 2), 0])
    for i in row_order[1:]:
        mbconv_row(i)
    weights[2].wait()
    weights[3].wait()
    kind_order = list(dict.fromkeys(i % kinds for i in row_order))
    for kind in kind_order:
        attend(kind)
    for kind in kind_order:
        finish(kind)

    for i, (sends, *_) in enumerate(halos):

        @pl.when(sends)
        def _():
            halo_copy(i).wait_send()

    def drain(n, carry):
        other = lax.rem(own + n, team)
        for kind in range(kinds):
            for step in range(per_kind):
                forward_copy(kind, step, other, own).wait_send()
            for g in range(group_count):
                back_copy(kind, g, other, own).wait_send()
        return carry

    lax.fori_loop(1, team, drain, 0)


def local(
    tokens, expand_weight, depth_kernel, project_weight, norm_gain, attend_weight, output_weight
):
    tile_rows, tile_cols, channels = tokens.shape
    hidden = expand_weight.shape[1]
    row_count = lax.axis_size("row")
    col_count = lax.axis_size("col")
    stride_rows = tile_rows * row_count // GRID
    stride_cols = tile_cols * col_count // GRID
    blocks = tile_cols // stride_cols
    spread = max(1, stride_rows // tile_rows)
    kinds = min(stride_rows, tile_rows)
    per_kind = tile_rows // kinds
    team = row_count // spread * col_count
    piece = stride_cols // team * blocks
    row_order = [i for i in range(1, tile_rows) if i % kinds == 1 % kinds]
    row_order += [i for i in range(tile_rows - 1, -1, -1) if i not in row_order]
    bf16, f32 = jnp.bfloat16, jnp.float32
    exchange = (kinds, per_kind, team, piece, channels)
    returned = (kinds, piece // blocks, team, per_kind * blocks, channels)
    out = pl.pallas_call(
        functools.partial(kernel, row_count, col_count, spread, blocks, row_order),
        out_shape=jax.ShapeDtypeStruct((tile_rows, tile_cols, channels), bf16),
        in_specs=[pl.BlockSpec(memory_space=pltpu.VMEM)] * 3
        + [pl.BlockSpec(memory_space=pl.ANY)] * 4,
        out_specs=pl.BlockSpec(memory_space=pltpu.VMEM),
        scratch_shapes=[
            pltpu.VMEM(expand_weight.shape, bf16),
            pltpu.VMEM(project_weight.shape, bf16),
            pltpu.VMEM(attend_weight.shape, bf16),
            pltpu.VMEM(output_weight.shape, bf16),
            pltpu.VMEM((2, tile_cols, channels), bf16),
            pltpu.VMEM((tile_rows + 2, 16, channels), bf16),
            pltpu.VMEM((tile_rows + 2, 16, channels), bf16),
            pltpu.VMEM((tile_cols, tile_cols), bf16),
            pltpu.VMEM((tile_rows + 2, tile_cols + 2 * blocks, channels), bf16),
            pltpu.VMEM((tile_rows + 2, stride_cols + 2, blocks, hidden), f32),
            pltpu.VMEM((tile_cols, hidden), bf16),
            pltpu.VMEM((tile_cols, channels), f32),
            pltpu.VMEM((tile_rows, tile_cols, channels), bf16),
            pltpu.VMEM(exchange, bf16),
            pltpu.VMEM(exchange, bf16),
            pltpu.VMEM((piece // blocks, channels, per_kind * team * blocks), bf16),
            pltpu.VMEM((piece // blocks, per_kind * team * blocks, channels), bf16),
            pltpu.VMEM((piece // blocks, channels, per_kind * team * blocks), bf16),
            pltpu.VMEM((channels, per_kind * team * blocks), f32),
            pltpu.VMEM(returned, bf16),
            pltpu.VMEM(returned, bf16),
            pltpu.SemaphoreType.DMA((4,)),
            pltpu.SemaphoreType.DMA((8,)),
            pltpu.SemaphoreType.DMA((8,)),
            pltpu.SemaphoreType.DMA((kinds, per_kind, team)),
            pltpu.SemaphoreType.DMA((kinds, per_kind, team)),
            pltpu.SemaphoreType.DMA((kinds, piece // blocks, team)),
            pltpu.SemaphoreType.DMA((kinds, piece // blocks, team)),
        ],
        compiler_params=pltpu.CompilerParams(
            collective_id=0, has_side_effects=True, vmem_limit_bytes=62 * 1024 * 1024
        ),
    )(
        tokens,
        depth_kernel,
        norm_gain.reshape(1, channels),
        expand_weight,
        project_weight,
        attend_weight,
        output_weight,
    )
    out = out.reshape(tile_rows, stride_cols, blocks, channels).transpose(0, 2, 1, 3)
    return out.reshape(tile_rows, tile_cols, channels)


def solution(mesh):
    placed = (P(("parts", "row"), "col", None), P(), P(), P(), P(), P(), P())
    return jax.shard_map(
        local,
        mesh=mesh,
        in_specs=placed,
        out_specs=P(("parts", "row"), "col", None),
        check_vma=False,
    )
```
